32 devices in a mesh: seq: 16 (over z, y, core), chan: 2 (over x).
Axes of the slice: x: 2, y: 2, z: 4, core: 2. Of those that a mesh axis runs over, the one named last changes fastest.
Arguments:
- tokens: bfloat16 [4096, 512], P('seq', 'chan'), may hold values from -6 to 6
- out_grad: bfloat16 [4096, 512], P('seq', 'chan'), may hold values from -6 to 6
- in_weight: bfloat16 [512, 1024], P('seq', 'chan'), may hold values from -0.25 to 0.25
- dt_weight: bfloat16 [512, 16], P('seq', 'chan'), may hold values from -0.25 to 0.25
- bc_weight: bfloat16 [512, 128], P('seq'), may hold values from -0.0625 to 0.0625
- out_weight: bfloat16 [1024, 512], P('chan', 'seq'), may hold values from -0.1875 to 0.1875
- decay_rate: float32 [2, 16], P(None, 'chan'), may hold values from 0.0014648438 to 8
- dt_bias: float32 [2, 16], P(None, 'chan'), may hold values from -5 to -4
- skip_gain: float32 [16], P('chan'), may hold values from 0.5 to 1.5
Outputs:
- tokens_grad: bfloat16 [4096, 512], P('seq', 'chan')
- in_weight_grad: float32 [512, 1024], P('seq', 'chan')
- dt_weight_grad: float32 [512, 16], P('seq', 'chan')
- bc_weight_grad: float32 [512, 128], P('seq')
- out_weight_grad: float32 [1024, 512], P('chan', 'seq')
- rate_grad: float32 [2, 16], P(None, 'chan')
- bias_grad: float32 [2, 16], P(None, 'chan')
- skip_grad: float32 [16], P('chan')
The draws below stay inside these ranges and needn't reach their ends.
All inputs are finite; a program needn't handle non-finite values.
Results may differ from the reference program's by a relative error of at most 0.0034.
Values may be sent and summed in bfloat16 or wider, within the bound.
A program may use at most 64 MiB of HBM per device.

```python
import math
import jax
import jax.numpy as jnp
from jax import lax

D = 512
E = 1024
STATE = 64
HEAD = 64
HEADS = 16
GROUP = 256
TOKENS = 4096


def draw_decay_rate(key, part):
    base_key = jax.random.fold_in(key, 11)
    mask_key, slow_key, fast_key = jax.random.split(base_key, 3)
    slow_share = 0.5
    slow_mask = jax.random.uniform(mask_key, (2, HEADS)) < slow_share
    slow_value = jnp.exp(jax.random.uniform(slow_key, (2, HEADS), minval=math.log(6.0), maxval=math.log(40.0))) / TOKENS
    fast_value = jnp.exp(jax.random.uniform(fast_key, (2, HEADS), minval=math.log(2.0), maxval=math.log(8.0)))
    return jnp.where(slow_mask, slow_value, fast_value).astype(jnp.float32)


def shard_levels(own_key, shape, cuts, smallest, high):
    def one(position, shards_of):
        draws = jax.random.uniform(jax.random.fold_in(jax.random.fold_in(own_key, 6), position), (shards_of,), jnp.float32, smallest / len(cuts), high / len(cuts))
        return jnp.repeat(jnp.exp(draws), shape[position] // shards_of).reshape((-1,) + (1,) * (len(shape) - position - 1))

    gain = one(*cuts[0])
    for cut in cuts[1:]:
        gain = gain * one(*cut)
    return gain


def scatter_about(rng, extent, scale, reach, cuts=(), held_as=jnp.bfloat16):
    values = jax.random.normal(rng, extent, jnp.float32) * scale
    if len(cuts) > 0:
        values = shard_levels(rng, extent, cuts, -0.22, 0.18) * values
    return jnp.clip(values, min=-reach, max=reach).astype(held_as)


def setup_inputs(seed: int = 0) -> dict:
    key_list = jax.random.split(jax.random.key(seed), 10)
    tokens = scatter_about(key_list[0], (TOKENS, D), 1.0, 6.0, ((0, 16), (1, 2)))
    out_grad = scatter_about(key_list[1], (TOKENS, D), 1.0, 6.0, ((0, 16), (1, 2)))
    in_weight = scatter_about(key_list[2], (D, E), D ** -0.5, 0.25, ((0, 16), (1, 2)))
    dt_weight = scatter_about(key_list[3], (D, HEADS), D ** -0.5, 0.25, ((0, 16), (1, 2)))
    bc_weight = scatter_about(key_list[4], (D, 2 * STATE), (D * 16) ** -0.5, 0.0625, ((0, 16),))
    out_weight = scatter_about(key_list[5], (E, D), E ** -0.5, 0.1875, ((0, 2), (1, 16)))
    decay_rate = draw_decay_rate(jax.random.fold_in(key_list[9], 71), 0)
    dt_bias = jnp.clip(-5.0 + 1.0 * jax.random.uniform(key_list[7], (2, HEADS), jnp.float32) ** shard_levels(key_list[7], (2, HEADS), ((1, 2),), -0.2, 0.2), -5.0, -4.0)
    skip_gain = jnp.clip(0.5 + 1.0 * jax.random.uniform(key_list[8], (HEADS,), jnp.float32) ** shard_levels(key_list[8], (HEADS,), ((0, 2),), -0.2, 0.2), 0.5, 1.5)
    return {"tokens": tokens, "out_grad": out_grad, "in_weight": in_weight, "dt_weight": dt_weight, "bc_weight": bc_weight, "out_weight": out_weight, "decay_rate": decay_rate, "dt_bias": dt_bias, "skip_gain": skip_gain}


def ssd_core(gated, step_size, b_proj, c_proj, rate, skip_gain, start_state):
    length, width = gated.shape
    heads = step_size.shape[1]
    head_dim = width // heads
    blocks = length // GROUP
    log_decay = -rate[None, :] * step_size
    driven = gated.reshape(length, heads, head_dim) * step_size[:, :, None]
    causal = lax.broadcasted_iota(jnp.int32, (GROUP, GROUP), 0) >= lax.broadcasted_iota(jnp.int32, (GROUP, GROUP), 1)

    def advance(memory, block):
        plain, pushed, decays, b_block, c_block = block
        running = jnp.cumsum(decays, axis=0)
        across = running.T
        spread = across[:, :, None] - across[:, None, :]
        kept = jnp.where(causal[None], jnp.exp(jnp.where(causal[None], spread, 0.0)), 0.0)
        scores = jnp.dot(c_block, b_block.T, precision=lax.Precision.HIGHEST)
        weighted = kept * scores[None]
        within = jnp.einsum('hts,shp->thp', weighted, pushed, precision=lax.Precision.HIGHEST)
        carried = jnp.einsum('tn,hpn->thp', c_block, memory, precision=lax.Precision.HIGHEST) * jnp.exp(running)[:, :, None]
        output = within + carried + skip_gain[None, :, None] * plain
        tail_decay = jnp.exp(running[-1][None, :] - running)
        memory = jnp.exp(running[-1])[:, None, None] * memory + jnp.einsum('sh,shp,sn->hpn', tail_decay, pushed, b_block, precision=lax.Precision.HIGHEST)
        return (memory, output.reshape(GROUP, width))
    final_state, outputs = lax.scan(jax.checkpoint(advance), start_state, (gated.reshape(blocks, GROUP, heads, head_dim), driven.reshape(blocks, GROUP, heads, head_dim), log_decay.reshape(blocks, GROUP, heads), b_proj.reshape(blocks, GROUP, b_proj.shape[1]), c_proj.reshape(blocks, GROUP, c_proj.shape[1])))
    return (outputs.reshape(length, width), final_state)

def one_direction(inputs, cotangent, in_weight, dt_weight, bc_weight, out_weight, rate, bias, skip_gain):
    packed = jnp.concatenate([in_weight, dt_weight, bc_weight], 1)
    projected = jnp.dot(inputs, packed, preferred_element_type=jnp.float32)
    preact = projected[:, :E]
    dt_pre = projected[:, E:E + HEADS] + bias[None, :]
    bc_proj = projected[:, E + HEADS:]
    gated = jax.nn.silu(preact)
    step_size = jax.nn.softplus(dt_pre)
    output_adjoint = jnp.dot(cotangent, out_weight.T, preferred_element_type=jnp.float32)
    start_state = jnp.zeros((HEADS, HEAD, STATE), jnp.float32)

    def core_only(gated_in, step_in, bc_in, rate_in, gain_in):
        return ssd_core(gated_in, step_in, bc_in[:, :STATE], bc_in[:, STATE:], rate_in, gain_in, start_state)[0]
    mixed, pullback = jax.vjp(core_only, gated, step_size, bc_proj, rate, skip_gain)
    d_gated, d_step, d_bc, d_rate, d_skip = pullback(output_adjoint)
    sig_pre = jax.nn.sigmoid(preact)
    d_pre = d_gated * sig_pre * (1.0 + preact * (1.0 - sig_pre))
    d_z = d_step * jax.nn.sigmoid(dt_pre)
    leading_gradient = jnp.concatenate([d_pre, d_z], 1).astype(jnp.bfloat16)
    primary_weight = jnp.concatenate([in_weight, dt_weight], 1)
    input_grad = jnp.dot(leading_gradient, primary_weight.T, preferred_element_type=jnp.float32) + jnp.dot(d_bc, bc_weight.astype(jnp.float32).T, precision=lax.Precision.HIGHEST)
    front_grad = jnp.dot(inputs.T, leading_gradient, preferred_element_type=jnp.float32)
    bc_grad = jnp.dot(inputs.astype(jnp.float32).T, d_bc, precision=lax.Precision.HIGHEST)
    out_grad_w = jnp.dot(mixed.astype(jnp.bfloat16).T, cotangent, preferred_element_type=jnp.float32)
    return (input_grad, front_grad, bc_grad, out_grad_w, d_rate * rate, lax.optimization_barrier(jnp.sum(d_z, axis=0)), d_skip)

def reference(tokens, out_grad, in_weight, dt_weight, bc_weight, out_weight, decay_rate, dt_bias, skip_gain):
    grad_scale = TOKENS ** (-0.5)
    forward = one_direction(tokens, out_grad, in_weight, dt_weight, bc_weight, out_weight, decay_rate[0], dt_bias[0], skip_gain)
    backward = one_direction(tokens[::-1], out_grad[::-1], in_weight, dt_weight, bc_weight, out_weight, decay_rate[1], dt_bias[1], skip_gain)
    tokens_grad = (forward[0] + backward[0][::-1]).astype(jnp.bfloat16)
    front_total = grad_scale * (forward[1] + backward[1])
    in_weight_grad = front_total[:, :E]
    dt_weight_grad = front_total[:, E:]
    bc_weight_grad = grad_scale * (forward[2] + backward[2])
    out_weight_grad = grad_scale * (forward[3] + backward[3])
    rate_grad = grad_scale * jnp.stack([forward[4], backward[4]])
    bias_grad = grad_scale * jnp.stack([forward[5], backward[5]])
    skip_grad = grad_scale * (forward[6] + backward[6])
    return (tokens_grad, in_weight_grad, dt_weight_grad, bc_weight_grad, out_weight_grad, rate_grad, bias_grad, skip_grad)
```

```python
import functools

import jax
import jax.numpy as jnp
from jax import lax
from jax.experimental import pallas as pl
from jax.experimental.pallas import tpu as pltpu
from jax.sharding import PartitionSpec as P

LANES = 128
F32, BF16 = jnp.float32, jnp.bfloat16
NN = (((1,), (0,)), ((), ()))
NT = (((1,), (1,)), ((), ()))
TN = (((0,), (0,)), ((), ()))


def dot(a, b, dims=NN):
    return lax.dot_general(a, b, dims, preferred_element_type=F32)


def dot32(a, b, dims=NN):
    return lax.dot_general(a, b, dims, precision=lax.Precision.HIGHEST, preferred_element_type=F32)


def halves(a):
    high = a.astype(BF16)
    return high, (a - high.astype(F32)).astype(BF16)


def dot3(a, b, dims=NN):
    return dot(a[0], b[0], dims) + (dot(a[0], b[1], dims) + dot(a[1], b[0], dims))


def kernel(
    sizes, own_ref, w_ref, vec_ref,
    tg_ref, iw_ref, dw_ref, bw_ref, ow_ref, small_ref,
    ubuf, wbuf, st, rs, po, cin, lg, gbuf, grecv, dbc_own, dbc_recv, sm, acc, sbuf, rbuf,
    u_send, u_recv, w_send, w_recv, a_send, a_recv, l_send, l_recv, b_send, b_recv,
    g_send, g_recv, d_send, d_recv, s_send, s_recv, r_send, r_recv,
):
    n, nc, T, cols, rows, width, heads, state, scale = sizes
    nb = n.bit_length() - 1
    head = width // heads
    front = width + LANES
    me, mc = lax.axis_index("seq"), lax.axis_index("chan")

    def flip(bit):
        return (1 << bit) * (1 - 2 * ((me // (1 << bit)) % 2))

    def flips(bits, subset):
        total = me
        for place, bit in enumerate(bits):
            if (subset >> place) & 1:
                total = total + flip(bit)
        return total

    def copy(src, dst, ssem, rsem, seq=None, chan=None):
        return pltpu.make_async_remote_copy(
            src_ref=src, dst_ref=dst, send_sem=ssem, recv_sem=rsem,
            device_id=(me if seq is None else seq, mc if chan is None else chan),
            device_id_type=pl.DeviceIdType.MESH,
        )

    barrier = pltpu.get_barrier_semaphore()
    for d in range(1, n):
        pl.semaphore_signal(barrier, inc=1, device_id=(lax.rem(me + d, n), mc), device_id_type=pl.DeviceIdType.MESH)
    for d in range(1, nc):
        pl.semaphore_signal(barrier, inc=1, device_id=(me, lax.rem(mc + d, nc)), device_id_type=pl.DeviceIdType.MESH)
    pl.semaphore_wait(barrier, n - 1 + nc - 1)

    u_copies = []
    for d in range(1, nc):
        c = copy(own_ref, ubuf.at[mc], u_send.at[d - 1], u_recv.at[d - 1], chan=lax.rem(mc + d, nc))
        c.start()
        u_copies.append(c)
    order = list(range(nb - 1, -1, -1))
    w_copies = []
    for i, bit in enumerate(order):
        for m in range(1 << i):
            number = (1 << i) - 1 + m
            block = flips(order[:i], m)
            if m:
                top = m.bit_length() - 1
                if top == i - 1:
                    w_copies[(1 << top) - 1 + (m - (1 << top))].wait_recv()
            c = copy(
                w_ref if m == 0 else wbuf.at[block], wbuf.at[block],
                w_send.at[number], w_recv.at[number], seq=me + flip(bit),
            )
            c.start()
            w_copies.append(c)
    ubuf[mc] = own_ref[...]
    wbuf[me] = w_ref[...]
    for c in u_copies:
        c.wait_recv()
    for c in w_copies[(1 << (nb - 1)) - 1 :]:
        c.wait_recv()

    w_all = wbuf[...].reshape(n * rows, 2 * width + 2 * LANES)
    proj = jnp.zeros((T, front + LANES), F32)
    q = jnp.zeros((T, width), F32)
    for c in range(nc):
        part = w_all[c * cols : (c + 1) * cols]
        proj = proj + dot(ubuf[c, 0], part[:, : front + LANES])
        q = q + dot(ubuf[c, 1], part[:, front + LANES :])
    pre, z, bc = proj[:, :width], proj[:, width:front], proj[:, front:]
    b_in, c_in = bc[:, :state], bc[:, state:]
    sig = 1.0 / (1.0 + jnp.exp(-pre))
    gated = pre * sig
    slope = sig * (1.0 + pre * (1.0 - sig))
    lane_head = lax.broadcasted_iota(jnp.int32, (LANES, width), 1) // head
    expand = (lane_head == lax.broadcasted_iota(jnp.int32, (LANES, width), 0)).astype(F32)
    row_i = lax.broadcasted_iota(jnp.int32, (T, T), 0)
    col_i = lax.broadcasted_iota(jnp.int32, (T, T), 1)
    lower, upper = row_i >= col_i, row_i <= col_i
    masks = (lower, upper)
    vec = vec_ref[...]
    rates = [vec[r : r + 1] for r in range(2)]
    skip = dot32(vec[4:5] + jnp.zeros((8, LANES), F32), expand)[0:1]
    b_h, c_h, q_h = halves(b_in), halves(c_in), halves(q)

    steps, zs, runs, totals, xs, e_run, e_tail = [], [], [], [], [], [], []
    pushes, pulls = [], []
    for r in range(2):
        zr = z + vec[2 + r : 3 + r]
        step = jnp.maximum(zr, 0.0) + jnp.log1p(jnp.exp(-jnp.abs(zr)))
        decay = -rates[r] * step
        run = dot32(masks[r].astype(F32), decay)
        total = run[T - 1 : T] if r == 0 else run[0:1]
        er = dot32(jnp.exp(run), expand)
        et = dot32(jnp.exp(total - run), expand)
        x = gated * dot32(step, expand)
        pushes.append(dot3(b_h, halves(et * x), TN))
        pulls.append(dot3(c_h, halves(er * q), TN))
        for held, value in ((steps, step), (zs, zr), (runs, run), (totals, total), (xs, x), (e_run, er), (e_tail, et)):
            held.append(value)
    per = 4 * state // n
    stacked = jnp.concatenate([pushes[0], pulls[1], pulls[0], pushes[1]], 0)
    st[...] = stacked.reshape(n, per, width).astype(st.dtype)
    lg[me] = jnp.concatenate([totals[0], totals[1], jnp.zeros((6, LANES), F32)], 0)
    rs[me] = st[me]
    a_copies = []
    for d in range(1, n):
        to = lax.rem(me + d, n)
        c = copy(lg.at[me], lg.at[me], l_send.at[d - 1], l_recv.at[d - 1], seq=to)
        c.start()
        e = copy(st.at[to], rs.at[me], a_send.at[d - 1], a_recv.at[d - 1], seq=to)
        e.start()
        a_copies += [c, e]

    score = dot3(c_h, b_h, NT)
    run_rows = [runs[r].T for r in range(2)]
    xh = [halves(xs[r]) for r in range(2)]
    outer = jnp.zeros((T, T), F32)
    within = [[], []]
    back = [[], []]

    def inside(r, outer):
        for j in range(heads):
            lanes = slice(j * head, (j + 1) * head)
            spread = runs[r][:, j : j + 1] - run_rows[r][j : j + 1, :]
            kept = jnp.where(masks[r], jnp.exp(jnp.where(masks[r], spread, 0.0)), 0.0)
            weighted = halves(kept * score)
            qj = (q_h[0][:, lanes], q_h[1][:, lanes])
            xj = (xh[r][0][:, lanes], xh[r][1][:, lanes])
            within[r].append(dot3(weighted, xj))
            back[r].append(dot3(weighted, qj, TN))
            outer = outer + kept * dot3(qj, xj, NT)
        return outer

    outer = inside(0, outer)

    for c in a_copies:
        c.wait_recv()
    decays = jnp.exp(dot32(lg[...].reshape(n * 8, LANES), expand)).reshape(n, 8, width)
    down = me // (n // 2)
    way = ((me * per) // state % 2).astype(F32)
    lane_dec = decays[:, 0:1] * (1.0 - way) + decays[:, 1:2] * way
    down_f = down.astype(F32)
    running = jnp.zeros((per, width), F32)
    for s in range(n):
        i = s * (1 - down) + (n - 1 - s) * down
        po[i] = running.astype(po.dtype)
        factor = lane_dec[s] * (1.0 - down_f) + lane_dec[n - 1 - s] * down_f
        running = factor * running + rs[i].astype(F32)
    cin[me] = po[me]
    b_copies = []
    for d in range(1, n):
        to = lax.rem(me + d, n)
        c = copy(po.at[to], cin.at[me], b_send.at[d - 1], b_recv.at[d - 1], seq=to)
        c.start()
        b_copies.append(c)

    outer = inside(1, outer)
    for c in b_copies:
        c.wait_recv()
    carried_all = cin[...].astype(F32).reshape(4, state, width)
    starts = (carried_all[0], carried_all[3])
    ends = (carried_all[2], carried_all[1])

    outer_h = halves(outer)
    d_c = dot3(outer_h, b_h)
    d_b = dot3(outer_h, c_h, TN)
    d_fronts, lows, small_rows = [], [], []
    bias_rows = []
    d_skip = dot32(jnp.sum(q * gated, axis=0, keepdims=True) + jnp.zeros((8, width), F32), expand, NT)[0:1] * 2.0
    for r in range(2):
        s_h, e_h = halves(starts[r]), halves(ends[r])
        y = jnp.concatenate(within[r], 1) + e_run[r] * dot3(c_h, s_h)
        tail_dx = e_tail[r] * dot3(b_h, e_h)
        dx = jnp.concatenate(back[r], 1) + tail_dx
        d_c = d_c + dot3(halves(e_run[r] * q), s_h, NT)
        d_b = d_b + dot3(halves(e_tail[r] * xs[r]), e_h, NT)
        mixed = y + skip * gated
        lows.append(mixed.astype(BF16))
        d_run = dot32(q * y - xs[r] * dx, expand, NT)
        ends_sum = jnp.sum(xs[r] * tail_dx, axis=0, keepdims=True)
        keep_row = e_run[r][T - 1 : T] if r == 0 else e_run[r][0:1]
        ends_sum = ends_sum + jnp.sum(ends[r] * starts[r] * keep_row, axis=0, keepdims=True)
        d_total = dot32(ends_sum + jnp.zeros((8, width), F32), expand, NT)[0:1]
        d_decay = dot32(masks[1 - r].astype(F32), d_run) + d_total
        step_wide = dot32(steps[r], expand)
        d_gated = skip * q + step_wide * dx
        d_step = dot32(gated * dx, expand, NT) - rates[r] * d_decay
        d_z = d_step / (1.0 + jnp.exp(-zs[r]))
        small_rows.append(-rates[r] * jnp.sum(steps[r] * d_decay, axis=0, keepdims=True))
        bias_rows.append(jnp.sum(d_z, axis=0, keepdims=True))
        d_fronts.append(jnp.concatenate([d_gated * slope, d_z], 1).astype(BF16))
    d_bc = jnp.concatenate([d_b, d_c], 1)
    dbc_own[...] = d_bc
    sm[me] = scale * jnp.concatenate(small_rows + bias_rows + [d_skip, jnp.zeros((3, LANES), F32)], 0)
    d_copies = []
    for d in range(1, nc):
        c = copy(dbc_own, dbc_recv.at[d - 1], d_send.at[d - 1], d_recv.at[d - 1], chan=lax.rem(mc + d, nc))
        c.start()
        d_copies.append(c)
    s_copies = []
    for d in range(1, n):
        c = copy(sm.at[me], sm.at[me], s_send.at[d - 1], s_recv.at[d - 1], seq=lax.rem(me + d, n))
        c.start()
        s_copies.append(c)

    dbc_h = halves(d_bc)
    w_all = wbuf[...].reshape(n * rows, 2 * width + 2 * LANES)
    for c in range(nc):
        part = w_all[c * cols : (c + 1) * cols]
        lead, maps = part[:, :front], part[:, front : front + LANES]
        g = dot(d_fronts[0], lead, NT) + dot(d_fronts[1], lead, NT)
        gbuf[c] = g + (dot(dbc_h[0], maps, NT) + dot(dbc_h[1], maps, NT))
    g_copies = []
    for d in range(1, nc):
        to = lax.rem(mc + d, nc)
        c = copy(gbuf.at[to], grecv.at[d - 1], g_send.at[d - 1], g_recv.at[d - 1], chan=to)
        c.start()
        g_copies.append(c)

    for c in d_copies:
        c.wait_recv()
    for d in range(1, nc):
        d_bc = d_bc + dbc_recv[d - 1]
    dbc_h = halves(d_bc)
    per_chan = cols // rows
    for c in range(nc):
        u, cot = ubuf[c, 0], ubuf[c, 1]
        lead = dot(u, d_fronts[0], TN) + dot(u, d_fronts[1], TN)
        maps = dot(u, dbc_h[0], TN) + dot(u, dbc_h[1], TN)
        outs = dot(cot, lows[0], TN) + dot(cot, lows[1], TN)
        packed = scale * jnp.concatenate([lead, maps, outs], 1)
        acc[c * per_chan : (c + 1) * per_chan] = packed.reshape(per_chan, rows, 2 * width + 2 * LANES)
    number = 0
    r_copies = []
    for bit in range(nb):
        higher = list(range(bit + 1, nb))
        first = number
        for m in range(1 << len(higher)):
            block = flips(higher, m) + flip(bit)
            sbuf[number] = acc[block].astype(BF16)
            c = copy(sbuf.at[number], rbuf.at[number], r_send.at[number], r_recv.at[number], seq=me + flip(bit))
            c.start()
            r_copies.append(c)
            number += 1
        for m in range(1 << len(higher)):
            r_copies[first + m].wait_recv()
            block = flips(higher, m)
            acc[block] = acc[block] + rbuf[first + m].astype(F32)
    done = acc[me]
    iw_ref[...] = done[:, :width]
    dw_ref[...] = done[:, width : width + heads]
    bw_ref[...] = done[:, front : front + LANES]
    ow_ref[...] = done[:, front + LANES :]
    for c in g_copies:
        c.wait_recv()
    g = gbuf[mc]
    for d in range(1, nc):
        g = g + grecv[d - 1]
    tg_ref[...] = g.astype(BF16)
    for c in s_copies:
        c.wait_recv()
    total = sm[0]
    for i in range(1, n):
        total = total + sm[i]
    small_ref[...] = total
    for c in u_copies + w_copies + a_copies + b_copies + d_copies + s_copies + g_copies + r_copies:
        c.wait_send()


def body(n, nc, tokens, out_grad, in_weight, dt_weight, bc_weight, out_weight, decay_rate, dt_bias, skip_gain):
    T, cols = tokens.shape
    rows, width = in_weight.shape
    heads = dt_weight.shape[1]
    state = bc_weight.shape[1] // 2
    scale = float(T * n) ** -0.5
    own = jnp.stack([tokens, out_grad])
    dt_wide = jnp.pad(dt_weight, ((0, 0), (0, LANES - heads)))
    packed = jnp.concatenate([in_weight, dt_wide, bc_weight, out_weight.T], 1)
    total_w = packed.shape[1]
    vec = jnp.pad(
        jnp.concatenate([decay_rate, dt_bias, skip_gain[None]], 0), ((0, 3), (0, LANES - heads))
    )
    per = 4 * state // n
    dma = pltpu.SemaphoreType.DMA
    seq_sems, chan_sems = dma((n - 1,)), dma((nc - 1,))
    vmem = pl.BlockSpec(memory_space=pltpu.VMEM)
    sizes = (n, nc, T, cols, rows, width, heads, state, scale)
    tg, iw, dw, bw, ow, small = pl.pallas_call(
        functools.partial(kernel, sizes),
        out_shape=(
            jax.ShapeDtypeStruct((T, cols), BF16),
            jax.ShapeDtypeStruct((rows, width), F32),
            jax.ShapeDtypeStruct((rows, heads), F32),
            jax.ShapeDtypeStruct((rows, 2 * state), F32),
            jax.ShapeDtypeStruct((rows, width), F32),
            jax.ShapeDtypeStruct((8, LANES), F32),
        ),
        in_specs=[vmem] * 3,
        out_specs=(vmem,) * 6,
        scratch_shapes=[
            pltpu.VMEM((nc, 2, T, cols), BF16),
            pltpu.VMEM((n, rows, total_w), BF16),
            pltpu.VMEM((n, per, width), F32),
            pltpu.VMEM((n, per, width), F32),
            pltpu.VMEM((n, per, width), F32),
            pltpu.VMEM((n, per, width), F32),
            pltpu.VMEM((n, 8, LANES), F32),
            pltpu.VMEM((nc, T, cols), F32),
            pltpu.VMEM((nc - 1, T, cols), F32),
            pltpu.VMEM((T, 2 * state), F32),
            pltpu.VMEM((nc - 1, T, 2 * state), F32),
            pltpu.VMEM((n, 8, LANES), F32),
            pltpu.VMEM((n, rows, total_w), F32),
            pltpu.VMEM((n - 1, rows, total_w), BF16),
            pltpu.VMEM((n - 1, rows, total_w), BF16),
            chan_sems, chan_sems, seq_sems, seq_sems, seq_sems, seq_sems, seq_sems, seq_sems, seq_sems, seq_sems,
            chan_sems, chan_sems, chan_sems, chan_sems, seq_sems, seq_sems, seq_sems, seq_sems,
        ],
        compiler_params=pltpu.CompilerParams(
            collective_id=0, has_side_effects=True, vmem_limit_bytes=48 * 1024 * 1024
        ),
        cost_estimate=pl.CostEstimate(flops=4 * 10**9, bytes_accessed=4 * 10**6, transcendentals=10**6),
    )(own, packed, vec)
    return (
        tg, iw, dw, bw, ow.T, small[0:2, :heads], small[2:4, :heads], small[4, :heads],
    )


def solution(mesh):
    in_specs = (
        P("seq", "chan"),
        P("seq", "chan"),
        P("seq", "chan"),
        P("seq", "chan"),
        P("seq", None),
        P("chan", "seq"),
        P(None, "chan"),
        P(None, "chan"),
        P("chan"),
    )
    out_specs = (
        P("seq", "chan"),
        P("seq", "chan"),
        P("seq", "chan"),
        P("seq", None),
        P("chan", "seq"),
        P(None, "chan"),
        P(None, "chan"),
        P("chan"),
    )
    local = functools.partial(body, mesh.shape["seq"], mesh.shape["chan"])
    return jax.shard_map(local, mesh=mesh, in_specs=in_specs, out_specs=out_specs, check_vma=False)
```

```python
import functools

import jax
import jax.numpy as jnp
from jax import lax
from jax.experimental import pallas as pl
from jax.experimental.pallas import tpu as pltpu
from jax.sharding import PartitionSpec as P

LANES = 128
F32, BF16 = jnp.float32, jnp.bfloat16
NN = (((1,), (0,)), ((), ()))
NT = (((1,), (1,)), ((), ()))
TN = (((0,), (0,)), ((), ()))


def dot(a, b, dims=NN):
    return lax.dot_general(a, b, dims, preferred_element_type=F32)


def dot32(a, b, dims=NN):
    return lax.dot_general(a, b, dims, precision=lax.Precision.HIGHEST, preferred_element_type=F32)


def halves(a):
    high = a.astype(BF16)
    return high, (a - high.astype(F32)).astype(BF16)


def dot3(a, b, dims=NN):
    return dot(a[0], b[0], dims) + (dot(a[0], b[1], dims) + dot(a[1], b[0], dims))


def kernel(
    sizes, tok_ref, og_ref, inw_ref, dtw_ref, bcw_ref, outw_ref, rate_ref, bias_ref, gain_ref,
    tg_ref, iw_ref, dw_ref, bw_ref, ow_ref, small_ref,
    ubuf, wbuf, st, rs, po, cin, lg, gbuf, grecv, dbc_own, dbc_recv, sm, vec_ref,
    acc_o, acc_l, first_o, first_l, sbuf_o, sbuf_l, rbuf_o, rbuf_l,
    u_send, u_recv, w_send, w_recv, a_send, a_recv, l_send, l_recv, b_send, b_recv,
    g_send, g_recv, d_send, d_recv, s_send, s_recv, o_send, o_recv, r_send, r_recv,
):
    n, nc, T, cols, rows, width, heads, state, scale = sizes
    nb = n.bit_length() - 1
    head = width // heads
    front = width + LANES
    me, mc = lax.axis_index("seq"), lax.axis_index("chan")

    def flip(bit):
        return (1 << bit) * (1 - 2 * ((me // (1 << bit)) % 2))

    def flips(bits, subset):
        total = me
        for place, bit in enumerate(bits):
            if (subset >> place) & 1:
                total = total + flip(bit)
        return total

    def copy(src, dst, ssem, rsem, seq=None, chan=None):
        return pltpu.make_async_remote_copy(
            src_ref=src, dst_ref=dst, send_sem=ssem, recv_sem=rsem,
            device_id=(me if seq is None else seq, mc if chan is None else chan),
            device_id_type=pl.DeviceIdType.MESH,
        )

    ubuf[mc, 0] = tok_ref[...]
    ubuf[mc, 1] = og_ref[...]
    eye = (
        lax.broadcasted_iota(jnp.int32, (width, width), 0) == lax.broadcasted_iota(jnp.int32, (width, width), 1)
    ).astype(BF16)
    wbuf[me, :, :width] = inw_ref[...]
    wbuf[me, :, width:front] = jnp.zeros((rows, LANES), BF16)
    wbuf[me, :, width : width + heads] = dtw_ref[...]
    wbuf[me, :, front : front + LANES] = bcw_ref[...]
    wbuf[me, :, front + LANES :] = dot(outw_ref[...], eye, TN).astype(BF16)
    vec_ref[...] = jnp.zeros((8, LANES), F32)
    vec_ref[0:2, :heads] = rate_ref[...]
    vec_ref[2:4, :heads] = bias_ref[...]
    vec_ref[4:5, :heads] = gain_ref[...]

    barrier = pltpu.get_barrier_semaphore()
    for d in range(1, n):
        pl.semaphore_signal(barrier, inc=1, device_id=(lax.rem(me + d, n), mc), device_id_type=pl.DeviceIdType.MESH)
    for d in range(1, nc):
        pl.semaphore_signal(barrier, inc=1, device_id=(me, lax.rem(mc + d, nc)), device_id_type=pl.DeviceIdType.MESH)
    pl.semaphore_wait(barrier, n - 1 + nc - 1)

    order = list(range(nb - 1, -1, -1))
    w_copies = {}

    def pass_on(m, after):
        block = flips(order, m)
        for i in range(after, nb):
            number = (1 << i) - 1 + m
            c = copy(wbuf.at[block], wbuf.at[block], w_send.at[number], w_recv.at[number], seq=me + flip(order[i]))
            c.start()
            w_copies[i, m] = c

    pass_on(0, 0)
    u_copies = []
    for d in range(1, nc):
        c = copy(ubuf.at[mc], ubuf.at[mc], u_send.at[d - 1], u_recv.at[d - 1], chan=lax.rem(mc + d, nc))
        c.start()
        u_copies.append(c)
    arrivals = sorted(((i, m) for i in range(nb) for m in range(1 << i)), key=lambda e: (e[1].bit_count(), e))
    for i, m in arrivals:
        w_copies[i, m].wait_recv()
        pass_on(m + (1 << i), i + 1)
    for c in u_copies:
        c.wait_recv()
    w_copies = list(w_copies.values())

    w_all = wbuf[...].reshape(n * rows, 2 * width + 2 * LANES)
    proj = jnp.zeros((T, front + LANES), F32)
    q = jnp.zeros((T, width), F32)
    for c in range(nc):
        part = w_all[c * cols : (c + 1) * cols]
        proj = proj + dot(ubuf[c, 0], part[:, : front + LANES])
        q = q + dot(ubuf[c, 1], part[:, front + LANES :])
    pre, z, bc = proj[:, :width], proj[:, width:front], proj[:, front:]
    b_in, c_in = bc[:, :state], bc[:, state:]
    sig = 1.0 / (1.0 + jnp.exp(-pre))
    gated = pre * sig
    slope = sig * (1.0 + pre * (1.0 - sig))
    per_chan = cols // rows
    priority = sorted(range(n // 2), key=lambda m: tuple(-((m >> p) & 1) for p in range(nb)))

    def begin(acc, first, send, recv, held):
        for m in priority:
            block = flips(range(1, nb), m) + flip(0)
            c = copy(acc.at[block], first.at[m], send.at[m], recv.at[m], seq=me + flip(0))
            c.start()
            held[0, m] = c

    def advance(bit, acc, first, sbuf, rbuf, send, recv, held):
        base = n - (n >> bit)
        for m in (m for m in priority if m < (n >> (bit + 1))):
            held[bit, m].wait_recv()
            block = flips(range(bit + 1, nb), m)
            got = first[m] if bit == 0 else rbuf[base - n // 2 + m].astype(F32)
            value = acc[block] + got
            if m & 1:
                number = n - (n >> (bit + 1)) + (m >> 1)
                slot = number - n // 2
                sbuf[slot] = value.astype(BF16)
                c = copy(sbuf.at[slot], rbuf.at[slot], send.at[number], recv.at[number], seq=me + flip(bit + 1))
                c.start()
                held[bit + 1, m >> 1] = c
            else:
                acc[block] = value

    o_held, l_held = {}, {}
    o_args = (acc_o, first_o, sbuf_o, rbuf_o, o_send, o_recv, o_held)
    l_args = (acc_l, first_l, sbuf_l, rbuf_l, r_send, r_recv, l_held)
    lane_head = lax.broadcasted_iota(jnp.int32, (LANES, width), 1) // head
    expand = (lane_head == lax.broadcasted_iota(jnp.int32, (LANES, width), 0)).astype(F32)
    row_i = lax.broadcasted_iota(jnp.int32, (T, T), 0)
    col_i = lax.broadcasted_iota(jnp.int32, (T, T), 1)
    lower, upper = row_i >= col_i, row_i <= col_i
    masks = (lower, upper)
    vec = vec_ref[...]
    rates = [vec[r : r + 1] for r in range(2)]
    skip = dot32(vec[4:5] + jnp.zeros((8, LANES), F32), expand)[0:1]
    b_h, c_h, q_h = halves(b_in), halves(c_in), halves(q)

    steps, zs, runs, totals, xs, e_run, e_tail = [], [], [], [], [], [], []
    pushes, pulls = [], []
    for r in range(2):
        zr = z + vec[2 + r : 3 + r]
        step = jnp.maximum(zr, 0.0) + jnp.log1p(jnp.exp(-jnp.abs(zr)))
        decay = -rates[r] * step
        run = dot32(masks[r].astype(F32), decay)
        total = run[T - 1 : T] if r == 0 else run[0:1]
        er = dot32(jnp.exp(run), expand)
        et = dot32(jnp.exp(total - run), expand)
        x = gated * dot32(step, expand)
        pushes.append(dot3(b_h, halves(et * x), TN))
        pulls.append(dot3(c_h, halves(er * q), TN))
        for held, value in ((steps, step), (zs, zr), (runs, run), (totals, total), (xs, x), (e_run, er), (e_tail, et)):
            held.append(value)
    per = 4 * state // n
    stacked = jnp.concatenate([pushes[0], pulls[1], pulls[0], pushes[1]], 0)
    st[...] = stacked.reshape(n, per, width).astype(st.dtype)
    lg[me] = jnp.concatenate([totals[0], totals[1], jnp.zeros((6, LANES), F32)], 0)
    rs[me] = st[me]
    a_copies = []
    for d in range(1, n):
        to = lax.rem(me + d, n)
        c = copy(lg.at[me], lg.at[me], l_send.at[d - 1], l_recv.at[d - 1], seq=to)
        c.start()
        e = copy(st.at[to], rs.at[me], a_send.at[d - 1], a_recv.at[d - 1], seq=to)
        e.start()
        a_copies += [c, e]

    score = dot3(c_h, b_h, NT)
    run_rows = [runs[r].T for r in range(2)]
    xh = [halves(xs[r]) for r in range(2)]
    outer = jnp.zeros((T, T), F32)
    within = [[], []]
    back = [[], []]

    def inside(r, outer):
        for j in range(heads):
            lanes = slice(j * head, (j + 1) * head)
            spread = runs[r][:, j : j + 1] - run_rows[r][j : j + 1, :]
            kept = jnp.where(masks[r], jnp.exp(jnp.where(masks[r], spread, 0.0)), 0.0)
            weighted = halves(kept * score)
            qj = (q_h[0][:, lanes], q_h[1][:, lanes])
            xj = (xh[r][0][:, lanes], xh[r][1][:, lanes])
            within[r].append(dot3(weighted, xj))
            back[r].append(dot3(weighted, qj, TN))
            outer = outer + kept * dot3(qj, xj, NT)
        return outer

    outer = inside(0, outer)

    for c in a_copies:
        c.wait_recv()
    decays = jnp.exp(dot32(lg[...].reshape(n * 8, LANES), expand)).reshape(n, 8, width)
    down = me // (n // 2)
    way = ((me * per) // state % 2).astype(F32)
    lane_dec = decays[:, 0:1] * (1.0 - way) + decays[:, 1:2] * way
    down_f = down.astype(F32)
    running = jnp.zeros((per, width), F32)
    for s in range(n):
        i = s * (1 - down) + (n - 1 - s) * down
        po[i] = running.astype(po.dtype)
        factor = lane_dec[s] * (1.0 - down_f) + lane_dec[n - 1 - s] * down_f
        running = factor * running + rs[i].astype(F32)
    cin[me] = po[me]
    b_copies = []
    for d in range(1, n):
        to = lax.rem(me + d, n)
        c = copy(po.at[to], cin.at[me], b_send.at[d - 1], b_recv.at[d - 1], seq=to)
        c.start()
        b_copies.append(c)

    outer = inside(1, outer)
    for c in b_copies:
        c.wait_recv()
    carried_all = cin[...].astype(F32).reshape(4, state, width)
    starts = (carried_all[0], carried_all[3])
    ends = (carried_all[2], carried_all[1])

    outer_h = halves(outer)
    d_c = dot3(outer_h, b_h)
    d_b = dot3(outer_h, c_h, TN)
    d_fronts, lows, small_rows = [], [], []
    bias_rows = []
    d_skip = dot32(jnp.sum(q * gated, axis=0, keepdims=True) + jnp.zeros((8, width), F32), expand, NT)[0:1] * 2.0
    ys, tails, dxs, s_hs, e_hs = [], [], [], [], []
    for r in range(2):
        s_h, e_h = halves(starts[r]), halves(ends[r])
        y = jnp.concatenate(within[r], 1) + e_run[r] * dot3(c_h, s_h)
        lows.append((y + skip * gated).astype(BF16))
        ys.append(y)
        s_hs.append(s_h)
        e_hs.append(e_h)
    for c in range(nc):
        cot = ubuf[c, 1]
        outs = scale * (dot(cot, lows[0], TN) + dot(cot, lows[1], TN))
        acc_o[c * per_chan : (c + 1) * per_chan] = outs.reshape(per_chan, rows, width)
    begin(acc_o, first_o, o_send, o_recv, o_held)
    for r in range(2):
        tail_dx = e_tail[r] * dot3(b_h, e_hs[r])
        tails.append(tail_dx)
        dxs.append(jnp.concatenate(back[r], 1) + tail_dx)
        d_c = d_c + dot3(halves(e_run[r] * q), s_hs[r], NT)
        d_b = d_b + dot3(halves(e_tail[r] * xs[r]), e_hs[r], NT)
    d_bc = jnp.concatenate([d_b, d_c], 1)
    dbc_own[...] = d_bc
    d_copies = []
    for d in range(1, nc):
        c = copy(dbc_own, dbc_recv.at[d - 1], d_send.at[d - 1], d_recv.at[d - 1], chan=lax.rem(mc + d, nc))
        c.start()
        d_copies.append(c)
    advance(0, *o_args)
    for r in range(2):
        y, tail_dx, dx = ys[r], tails[r], dxs[r]
        d_run = dot32(q * y - xs[r] * dx, expand, NT)
        ends_sum = jnp.sum(xs[r] * tail_dx, axis=0, keepdims=True)
        keep_row = e_run[r][T - 1 : T] if r == 0 else e_run[r][0:1]
        ends_sum = ends_sum + jnp.sum(ends[r] * starts[r] * keep_row, axis=0, keepdims=True)
        d_total = dot32(ends_sum + jnp.zeros((8, width), F32), expand, NT)[0:1]
        d_decay = dot32(masks[1 - r].astype(F32), d_run) + d_total
        d_gated = skip * q + dot32(steps[r], expand) * dx
        d_step = dot32(gated * dx, expand, NT) - rates[r] * d_decay
        d_z = d_step / (1.0 + jnp.exp(-zs[r]))
        small_rows.append(-rates[r] * jnp.sum(steps[r] * d_decay, axis=0, keepdims=True))
        bias_rows.append(jnp.sum(d_z, axis=0, keepdims=True))
        d_fronts.append(jnp.concatenate([d_gated * slope, d_z], 1).astype(BF16))
    sm[me] = scale * jnp.concatenate(small_rows + bias_rows + [d_skip, jnp.zeros((3, LANES), F32)], 0)
    s_copies = []
    for d in range(1, n):
        c = copy(sm.at[me], sm.at[me], s_send.at[d - 1], s_recv.at[d - 1], seq=lax.rem(me + d, n))
        c.start()
        s_copies.append(c)

    dbc_h = halves(d_bc)
    w_all = wbuf[...].reshape(n * rows, 2 * width + 2 * LANES)
    for c in range(nc):
        part = w_all[c * cols : (c + 1) * cols]
        lead, maps = part[:, :front], part[:, front : front + LANES]
        g = dot(d_fronts[0], lead, NT) + dot(d_fronts[1], lead, NT)
        gbuf[c] = g + (dot(dbc_h[0], maps, NT) + dot(dbc_h[1], maps, NT))
    g_copies = []
    for d in range(1, nc):
        to = lax.rem(mc + d, nc)
        c = copy(gbuf.at[to], grecv.at[d - 1], g_send.at[d - 1], g_recv.at[d - 1], chan=to)
        c.start()
        g_copies.append(c)

    for c in d_copies:
        c.wait_recv()
    for d in range(1, nc):
        d_bc = d_bc + dbc_recv[d - 1]
    dbc_h = halves(d_bc)
    for c in range(nc):
        u = ubuf[c, 0]
        lead = dot(u, d_fronts[0], TN) + dot(u, d_fronts[1], TN)
        maps = dot(u, dbc_h[0], TN) + dot(u, dbc_h[1], TN)
        packed = scale * jnp.concatenate([lead, maps], 1)
        acc_l[c * per_chan : (c + 1) * per_chan] = packed.reshape(per_chan, rows, front + LANES)
    begin(acc_l, first_l, r_send, r_recv, l_held)
    for bit in range(1, nb):
        advance(bit, *o_args)
        advance(bit - 1, *l_args)
    advance(nb - 1, *l_args)
    r_copies = list(o_held.values()) + list(l_held.values())
    done = acc_l[me]
    iw_ref[...] = done[:, :width]
    dw_ref[...] = done[:, width : width + heads]
    bw_ref[...] = done[:, front:]
    ow_ref[...] = acc_o[me]
    for c in g_copies:
        c.wait_recv()
    g = gbuf[mc]
    for d in range(1, nc):
        g = g + grecv[d - 1]
    tg_ref[...] = g.astype(BF16)
    for c in s_copies:
        c.wait_recv()
    total = sm[0]
    for i in range(1, n):
        total = total + sm[i]
    small_ref[...] = total
    for c in u_copies + w_copies + a_copies + b_copies + d_copies + s_copies + g_copies + r_copies:
        c.wait_send()


def body(n, nc, tokens, out_grad, in_weight, dt_weight, bc_weight, out_weight, decay_rate, dt_bias, skip_gain):
    T, cols = tokens.shape
    rows, width = in_weight.shape
    heads = dt_weight.shape[1]
    state = bc_weight.shape[1] // 2
    scale = float(T * n) ** -0.5
    total_w = 2 * width + 2 * LANES
    lead_w = width + 2 * LANES
    per = 4 * state // n
    dma = pltpu.SemaphoreType.DMA
    seq_sems, chan_sems = dma((n - 1,)), dma((nc - 1,))
    vmem = pl.BlockSpec(memory_space=pltpu.VMEM)
    sizes = (n, nc, T, cols, rows, width, heads, state, scale)
    tg, iw, dw, bw, ow, small = pl.pallas_call(
        functools.partial(kernel, sizes),
        out_shape=(
            jax.ShapeDtypeStruct((T, cols), BF16),
            jax.ShapeDtypeStruct((rows, width), F32),
            jax.ShapeDtypeStruct((rows, heads), F32),
            jax.ShapeDtypeStruct((rows, 2 * state), F32),
            jax.ShapeDtypeStruct((rows, width), F32),
            jax.ShapeDtypeStruct((8, LANES), F32),
        ),
        in_specs=[vmem] * 9,
        out_specs=(vmem,) * 6,
        scratch_shapes=[
            pltpu.VMEM((nc, 2, T, cols), BF16),
            pltpu.VMEM((n, rows, total_w), BF16),
            pltpu.VMEM((n, per, width), F32),
            pltpu.VMEM((n, per, width), F32),
            pltpu.VMEM((n, per, width), F32),
            pltpu.VMEM((n, per, width), F32),
            pltpu.VMEM((n, 8, LANES), F32),
            pltpu.VMEM((nc, T, cols), F32),
            pltpu.VMEM((nc - 1, T, cols), F32),
            pltpu.VMEM((T, 2 * state), F32),
            pltpu.VMEM((nc - 1, T, 2 * state), F32),
            pltpu.VMEM((n, 8, LANES), F32),
            pltpu.VMEM((8, LANES), F32),
            pltpu.VMEM((n, rows, width), F32),
            pltpu.VMEM((n, rows, lead_w), F32),
            pltpu.VMEM((n // 2, rows, width), F32),
            pltpu.VMEM((n // 2, rows, lead_w), F32),
            pltpu.VMEM((n // 2 - 1, rows, width), BF16),
            pltpu.VMEM((n // 2 - 1, rows, lead_w), BF16),
            pltpu.VMEM((n // 2 - 1, rows, width), BF16),
            pltpu.VMEM((n // 2 - 1, rows, lead_w), BF16),
            chan_sems, chan_sems, seq_sems, seq_sems, seq_sems, seq_sems, seq_sems, seq_sems, seq_sems, seq_sems,
            chan_sems, chan_sems, chan_sems, chan_sems, seq_sems, seq_sems, seq_sems, seq_sems, seq_sems, seq_sems,
        ],
        compiler_params=pltpu.CompilerParams(
            collective_id=0, has_side_effects=True, vmem_limit_bytes=48 * 1024 * 1024
        ),
        cost_estimate=pl.CostEstimate(flops=4 * 10**9, bytes_accessed=4 * 10**6, transcendentals=10**6),
    )(
        tokens, out_grad, in_weight, dt_weight, bc_weight, out_weight,
        decay_rate, dt_bias, skip_gain.reshape(1, heads),
    )
    return (
        tg, iw, dw, bw, ow.T, small[0:2, :heads], small[2:4, :heads], small[4, :heads],
    )


def solution(mesh):
    in_specs = (
        P("seq", "chan"),
        P("seq", "chan"),
        P("seq", "chan"),
        P("seq", "chan"),
        P("seq", None),
        P("chan", "seq"),
        P(None, "chan"),
        P(None, "chan"),
        P("chan"),
    )
    out_specs = (
        P("seq", "chan"),
        P("seq", "chan"),
        P("seq", "chan"),
        P("seq", None),
        P("chan", "seq"),
        P(None, "chan"),
        P(None, "chan"),
        P("chan"),
    )
    local = functools.partial(body, mesh.shape["seq"], mesh.shape["chan"])
    return jax.shard_map(local, mesh=mesh, in_specs=in_specs, out_specs=out_specs, check_vma=False)
```
